32 devices in a mesh: shard: 2 (over y), ctx: 4 (over x, core), tensor: 4 (over z).
Axes of the slice: x: 2, y: 2, z: 4, core: 2. Of those that a mesh axis runs over, the one named last changes fastest.
Arguments:
- tokens: bfloat16 [8, 1376, 1024], P('shard', 'ctx'), may hold values from -6 to 6
- cotangent: bfloat16 [8, 1376, 1024], P('shard', 'ctx'), may hold values from -6 to 6
- norm1_gain: bfloat16 [1024], P('shard'), may hold values from 0.25 to 1.75
- norm1_shift: bfloat16 [1024], P('shard'), may hold values from -2 to 2
- query_weight: bfloat16 [1024, 1024], P('shard', 'tensor'), may hold values from -0.1875 to 0.1875
- query_bias: bfloat16 [1024], P('tensor'), may hold values from -2 to 2
- key_weight: bfloat16 [1024, 1024], P('shard', 'tensor'), may hold values from -0.1875 to 0.1875
- value_weight: bfloat16 [1024, 1024], P('shard', 'tensor'), may hold values from -0.1875 to 0.1875
- value_bias: bfloat16 [1024], P('tensor'), may hold values from -2 to 2
- out_weight: bfloat16 [1024, 1024], P('tensor', 'shard'), may hold values from -3 to 3
- out_bias: bfloat16 [1024], P('shard'), may hold values from -2 to 2
- scale_attn: bfloat16 [1024], P('shard'), may hold values from 0.5 to 2
- norm2_gain: bfloat16 [1024], P('shard'), may hold values from 0.25 to 1.75
- norm2_shift: bfloat16 [1024], P('shard'), may hold values from -2 to 2
- up_weight: bfloat16 [1024, 4096], P('shard', 'tensor'), may hold values from -0.1875 to 0.1875
- up_bias: bfloat16 [4096], P('tensor'), may hold values from -2 to 2
- down_weight: bfloat16 [4096, 1024], P('tensor', 'shard'), may hold values from -0.09375 to 0.09375
- down_bias: bfloat16 [1024], P('shard'), may hold values from -2 to 2
- scale_mlp: bfloat16 [1024], P('shard'), may hold values from 0.5 to 2
Outputs:
- block_out: float32 [8, 1376, 1024], P('shard', 'ctx')
- tokens_grad: float32 [8, 1376, 1024], P('shard', 'ctx')
- norm1_gain_grad: float32 [1024], P('shard')
- norm1_shift_grad: float32 [1024], P('shard')
- query_weight_grad: float32 [1024, 1024], P('shard', 'tensor')
- query_bias_grad: float32 [1024], P('tensor')
- key_weight_grad: float32 [1024, 1024], P('shard', 'tensor')
- value_weight_grad: float32 [1024, 1024], P('shard', 'tensor')
- value_bias_grad: float32 [1024], P('tensor')
- out_weight_grad: float32 [1024, 1024], P('tensor', 'shard')
- out_bias_grad: float32 [1024], P('shard')
- scale_attn_grad: float32 [1024], P('shard')
- norm2_gain_grad: float32 [1024], P('shard')
- norm2_shift_grad: float32 [1024], P('shard')
- up_weight_grad: float32 [1024, 4096], P('shard', 'tensor')
- up_bias_grad: float32 [4096], P('tensor')
- down_weight_grad: float32 [4096, 1024], P('tensor', 'shard')
- down_bias_grad: float32 [1024], P('shard')
- scale_mlp_grad: float32 [1024], P('shard')
The draws below stay inside these ranges and needn't reach their ends.
All inputs are finite; a program needn't handle non-finite values.
Results may differ from the reference program's by a relative error of at most 0.012.
Values may be sent and summed in bfloat16 or wider, within the bound.
A program may use at most 192 MiB of HBM per device.

```python
import math
import jax
import jax.numpy as jnp
from jax import lax

D = 1024
H = 16
HD = 64
FF = 4096
IMAGES = 8
SEQ = 1376


def raised(values, key, source, target, parts, factor):
    def block_of(position):
        return (jnp.arange(values.shape[position]) // (values.shape[position] // parts)).reshape((-1,) + (1,) * (values.ndim - 1 - position))

    one_side = jax.random.permutation(key, parts)[block_of(target)]
    second = (block_of(target) + parts // 2) % parts
    return jnp.where((block_of(source) == one_side) | (block_of(source) == second), factor * values, values)


def shard_levels(own_key, extent, split, least, high):
    factor_of = 1.0
    for axis_at, parts in split:
        steps = jax.random.uniform(jax.random.fold_in(jax.random.fold_in(own_key, 6), axis_at), (parts,), jnp.float32, least / len(split), high / len(split))
        factor_of = factor_of * jnp.repeat(jnp.exp(steps), extent[axis_at] // parts).reshape((-1,) + (1,) * (len(extent) - 1 - axis_at))
    return factor_of


def bell_draw(stream_key, dims, scale, most, pieces=(), kind=jnp.bfloat16):
    factor_of = shard_levels(stream_key, dims, pieces, -0.22, 0.18) if pieces else 1.0
    array = jax.random.normal(stream_key, dims, jnp.float32) * scale * factor_of
    return jnp.minimum(jnp.maximum(array, -most), most).astype(kind)


def noise_with(own_key, shape, width, most, pieces, heavy, kind=jnp.bfloat16):
    entries = width * jax.random.normal(own_key, shape, jnp.float32)
    if pieces:
        entries = entries * shard_levels(own_key, shape, pieces, -0.22, 0.18)
    return jnp.clip(raised(entries, jax.random.fold_in(own_key, 3), *heavy), -most, most).astype(kind)


def setup_inputs(seed: int = 0) -> dict:
    seeds = jax.random.split(jax.random.key(seed), 20)
    return {
        "tokens": bell_draw(seeds[0], (IMAGES, SEQ, D), 1.0, 6.0, ((0, 2), (1, 4))),
        "cotangent": noise_with(seeds[1], (IMAGES, SEQ, D), 1.0, 6.0, ((0, 2), (1, 4)), (0, 2, 2, 2.0)),
        "norm1_gain": jnp.clip(1.0 + 0.15 * jax.random.normal(seeds[2], (D,), jnp.float32), 0.25, 1.75).astype(jnp.bfloat16),
        "norm1_shift": bell_draw(seeds[3], (D,), 0.3, 2.0, ((0, 2),)),
        "query_weight": bell_draw(seeds[4], (D, D), D ** -0.5, 0.1875, ((0, 2), (1, 4))),
        "query_bias": bell_draw(seeds[5], (D,), 0.3, 2.0, ((0, 4),)),
        "key_weight": bell_draw(seeds[6], (D, D), D ** -0.5, 0.1875, ((0, 2), (1, 4))),
        "value_weight": bell_draw(seeds[7], (D, D), D ** -0.5, 0.1875, ((0, 2), (1, 4))),
        "value_bias": bell_draw(seeds[8], (D,), 0.3, 2.0, ((0, 4),)),
        "out_weight": bell_draw(seeds[9], (D, D), (max(D // 256, 1)) ** -0.5, 3.0, ((0, 4), (1, 2))),
        "out_bias": bell_draw(seeds[10], (D,), 0.3, 2.0, ((0, 2),)),
        "scale_attn": jnp.clip(jnp.exp(math.log(2.0) - 1.3862944 * jax.random.uniform(seeds[11], (D,), jnp.float32) ** shard_levels(seeds[11], (D,), ((0, 2),), -0.2, 0.2)), 0.5, 2.0).astype(jnp.bfloat16),
        "norm2_gain": jnp.clip(1.0 + 0.15 * jax.random.normal(seeds[12], (D,), jnp.float32), 0.25, 1.75).astype(jnp.bfloat16),
        "norm2_shift": bell_draw(seeds[13], (D,), 0.3, 2.0, ((0, 2),)),
        "up_weight": bell_draw(seeds[14], (D, FF), D ** -0.5, 0.1875, ((0, 2), (1, 4))),
        "up_bias": bell_draw(seeds[15], (FF,), 0.3, 2.0, ((0, 4),)),
        "down_weight": bell_draw(seeds[16], (FF, D), FF ** -0.5, 0.09375, ((0, 4), (1, 2))),
        "down_bias": bell_draw(seeds[17], (D,), 0.3, 2.0, ((0, 2),)),
        "scale_mlp": jnp.clip(jnp.exp(math.log(2.0) - 1.3862944 * jax.random.uniform(seeds[18], (D,), jnp.float32) ** shard_levels(seeds[18], (D,), ((0, 2),), -0.2, 0.2)), 0.5, 2.0).astype(jnp.bfloat16),
    }


@jax.custom_vjp
def low(v):
    return lax.optimization_barrier(v.astype(jnp.bfloat16)).astype(jnp.float32)

@jax.custom_vjp
def low_back(v):
    return v

def low_keep(v):
    return (low(v), None)

def low_pass(kept, grad):
    return (grad,)

def back_keep(v):
    return (v, None)

def back_low(kept, grad):
    return (low(grad),)
low.defvjp(low_keep, low_pass)
low_back.defvjp(back_keep, back_low)

def layer_norm(values, norm_gain, norm_shift):
    center = values - lax.optimization_barrier(jnp.mean(values, -1, keepdims=True))
    inverse = lax.rsqrt(lax.optimization_barrier(jnp.mean(center * center, -1, keepdims=True)) + 1e-06)
    return center * inverse * norm_gain + norm_shift

def project(values, weight):
    return jnp.einsum('bsd,de->bse', values, weight, precision=lax.Precision.HIGHEST)

def attend(args):
    queries, keys, values = args
    query_h = queries.reshape(queries.shape[0], H, HD)
    key_h = keys.reshape(keys.shape[0], H, HD)
    value_h = values.reshape(values.shape[0], H, HD)
    scores = jnp.einsum('qhe,khe->hqk', query_h, key_h, precision=lax.Precision.HIGHEST) * HD ** (-0.5)
    scores = low_back(scores)
    probs = jax.nn.softmax(scores, axis=-1)
    mixed = jnp.einsum('hqk,khe->qhe', low(probs), value_h, precision=lax.Precision.HIGHEST)
    return mixed.reshape(queries.shape[0], H * HD)

def forward(tokens, norm1_gain, norm1_shift, query_weight, query_bias, key_weight, value_weight, value_bias, out_weight, out_bias, scale_attn, norm2_gain, norm2_shift, up_weight, up_bias, down_weight, down_bias, scale_mlp):
    hidden_one = low(layer_norm(tokens, norm1_gain, norm1_shift))
    queries = low(low_back(project(hidden_one, query_weight) + query_bias))
    keys = low(low_back(project(hidden_one, key_weight)))
    values = low(low_back(project(hidden_one, value_weight) + value_bias))
    mixed = lax.map(jax.checkpoint(attend), (queries, keys, values))
    mixed = low(low_back(mixed))
    branch = low_back(project(mixed, out_weight))
    between_rows = tokens + scale_attn * (branch + out_bias)
    hidden_two = low(layer_norm(between_rows, norm2_gain, norm2_shift))
    inner = low_back(project(hidden_two, up_weight) + up_bias)
    active = low(jax.nn.gelu(inner, approximate=False))
    branch_two = low_back(project(active, down_weight))
    return between_rows + scale_mlp * (branch_two + down_bias)

def reference(tokens, cotangent, norm1_gain, norm1_shift, query_weight, query_bias, key_weight, value_weight, value_bias, out_weight, out_bias, scale_attn, norm2_gain, norm2_shift, up_weight, up_bias, down_weight, down_bias, scale_mlp):
    params = [norm1_gain, norm1_shift, query_weight, query_bias, key_weight, value_weight, value_bias, out_weight, out_bias, scale_attn, norm2_gain, norm2_shift, up_weight, up_bias, down_weight, down_bias, scale_mlp]
    params = [item.astype(jnp.float32) for item in params]
    input_rows = tokens.astype(jnp.float32)
    result, backward = jax.vjp(forward, input_rows, *params)
    grads = backward(cotangent.astype(jnp.float32))
    return (result, grads[0], grads[1], grads[2], grads[3], grads[4], grads[5], grads[6], grads[7], grads[8], grads[9], grads[10], grads[11], grads[12], grads[13], grads[14], grads[15], grads[16], grads[17])
```

```python
from functools import partial

import jax
import jax.numpy as jnp
from jax import lax
from jax.experimental import pallas as pl
from jax.experimental.pallas import tpu as pltpu
from jax.sharding import PartitionSpec as P

HD = 64


EPSILON = 1e-06


def layer_norm_forward(values, norm_gain, norm_shift):
    center = values - jnp.mean(values, -1, keepdims=True)
    inverse = lax.rsqrt(jnp.mean(center * center, -1, keepdims=True) + EPSILON)
    normed = center * inverse
    return (normed * norm_gain + norm_shift, normed, inverse)


def layer_norm_backward(incoming_gradient, normed, inverse, norm_gain):
    scaled = incoming_gradient * norm_gain
    return inverse * (
        scaled
        - jnp.mean(scaled, -1, keepdims=True)
        - normed * jnp.mean(scaled * normed, -1, keepdims=True)
    )


def mat_mul(left, right):
    return jnp.dot(left, right, preferred_element_type=jnp.float32)


def rows_mul(left, right):
    return jnp.einsum("rd,re->de", left, right, preferred_element_type=jnp.float32)


def back_mul(left, right):
    return jnp.einsum("re,de->rd", left, right, preferred_element_type=jnp.float32)


def column_total_sum(values):
    return jnp.sum(values.astype(jnp.float32), 0)


def split_heads(values, heads):
    return values.reshape(values.shape[0], heads, HD)


def scores_of(queries, keys_all, heads):
    return jnp.einsum(
        "qhe,khe->hqk",
        split_heads(queries, heads),
        split_heads(keys_all, heads),
        preferred_element_type=jnp.float32,
    ) * HD ** (-0.5)


def attend_forward(heads, args):
    queries, keys_all, values_all = args
    scores = scores_of(queries, keys_all, heads)
    row_top = jnp.max(scores, -1, keepdims=True)
    expo = jnp.exp(scores - row_top)
    total = jnp.sum(expo, -1, keepdims=True)
    probs = (expo / total).astype(jnp.bfloat16)
    mixed = jnp.einsum(
        "hqk,khe->qhe", probs, split_heads(values_all, heads), preferred_element_type=jnp.float32
    )
    log_total = (row_top + jnp.log(total))[..., 0]
    return (mixed.reshape(queries.shape[0], heads * HD), log_total)


def attend_backward(heads, args):
    queries, keys_all, values_all, incoming_gradient, log_total = args
    scores = scores_of(queries, keys_all, heads)
    probs = jnp.exp(scores - log_total[..., None])
    up_heads = split_heads(incoming_gradient, heads)
    grad_value = jnp.einsum(
        "hqk,qhe->khe", probs.astype(jnp.bfloat16), up_heads, preferred_element_type=jnp.float32
    )
    grad_prob = jnp.einsum(
        "qhe,khe->hqk", up_heads, split_heads(values_all, heads), preferred_element_type=jnp.float32
    )
    grad_score = (probs * (grad_prob - jnp.sum(probs * grad_prob, -1, keepdims=True))).astype(
        jnp.bfloat16
    )
    grad_query = jnp.einsum(
        "hqk,khe->qhe", grad_score, split_heads(keys_all, heads), preferred_element_type=jnp.float32
    ) * HD ** (-0.5)
    grad_key = jnp.einsum(
        "hqk,qhe->khe", grad_score, split_heads(queries, heads), preferred_element_type=jnp.float32
    ) * HD ** (-0.5)
    width = heads * HD
    return (
        grad_query.reshape(queries.shape[0], width),
        grad_key.reshape(keys_all.shape[0], width),
        grad_value.reshape(keys_all.shape[0], width),
    )


def local(
    tokens,
    cotangent,
    norm1_gain,
    norm1_shift,
    query_weight,
    query_bias,
    key_weight,
    value_weight,
    value_bias,
    out_weight,
    out_bias,
    scale_attn,
    norm2_gain,
    norm2_shift,
    up_weight,
    up_bias,
    down_weight,
    down_bias,
    scale_mlp,
):
    full_g1, full_s1, full_wq, full_wk, full_wv, full_wo, full_bo, full_la = (
        lax.all_gather(norm1_gain, "shard", axis=0, tiled=True),
        lax.all_gather(norm1_shift, "shard", axis=0, tiled=True),
        lax.all_gather(query_weight, "shard", axis=0, tiled=True),
        lax.all_gather(key_weight, "shard", axis=0, tiled=True),
        lax.all_gather(value_weight, "shard", axis=0, tiled=True),
        lax.all_gather(out_weight, "shard", axis=1, tiled=True),
        lax.all_gather(out_bias, "shard", axis=0, tiled=True),
        lax.all_gather(scale_attn, "shard", axis=0, tiled=True),
    )
    full_g2, full_s2, full_wu, full_wd, full_bd, full_lm = (
        lax.all_gather(norm2_gain, "shard", axis=0, tiled=True),
        lax.all_gather(norm2_shift, "shard", axis=0, tiled=True),
        lax.all_gather(up_weight, "shard", axis=0, tiled=True),
        lax.all_gather(down_weight, "shard", axis=1, tiled=True),
        lax.all_gather(down_bias, "shard", axis=0, tiled=True),
        lax.all_gather(scale_mlp, "shard", axis=0, tiled=True),
    )
    first_norm_gain = full_g1.astype(jnp.float32)
    first_norm_offset = full_s1.astype(jnp.float32)
    second_norm_gain = full_g2.astype(jnp.float32)
    second_norm_offset = full_s2.astype(jnp.float32)
    bias_out = full_bo.astype(jnp.float32)
    layer_attn = full_la.astype(jnp.float32)
    bias_down = full_bd.astype(jnp.float32)
    layer_mlp = full_lm.astype(jnp.float32)
    img_count, tok_count, width = tokens.shape
    row_count = img_count * tok_count
    local_width = full_wq.shape[1]
    heads = local_width // HD
    input_rows = tokens.astype(jnp.float32).reshape(row_count, width)
    incoming_gradient = cotangent.astype(jnp.float32).reshape(row_count, width)
    first_normalized_rows, first_centered_scaled, first_inverse_deviation = layer_norm_forward(
        input_rows, first_norm_gain, first_norm_offset
    )
    hidden_one = first_normalized_rows.astype(jnp.bfloat16)
    queries = (mat_mul(hidden_one, full_wq) + query_bias.astype(jnp.float32)).astype(jnp.bfloat16)
    keys_local = mat_mul(hidden_one, full_wk).astype(jnp.bfloat16)
    values_local = (mat_mul(hidden_one, full_wv) + value_bias.astype(jnp.float32)).astype(
        jnp.bfloat16
    )
    keys_all, values_all = (
        lax.all_gather(
            keys_local.reshape(img_count, tok_count, local_width), "ctx", axis=1, tiled=True
        ),
        lax.all_gather(
            values_local.reshape(img_count, tok_count, local_width), "ctx", axis=1, tiled=True
        ),
    )
    query_img = queries.reshape(img_count, tok_count, local_width)
    mixed, log_total = lax.map(partial(attend_forward, heads), (query_img, keys_all, values_all))
    mixed_low = mixed.reshape(row_count, local_width).astype(jnp.bfloat16)
    branch = lax.psum(mat_mul(mixed_low, full_wo), "tensor")
    between_rows = input_rows + layer_attn * (branch + bias_out)
    second_normalized_rows, second_centered_scaled, second_inverse_deviation = layer_norm_forward(
        between_rows, second_norm_gain, second_norm_offset
    )
    hidden_two = second_normalized_rows.astype(jnp.bfloat16)
    inner = mat_mul(hidden_two, full_wu) + up_bias.astype(jnp.float32)
    active_low = jax.nn.gelu(inner, approximate=False).astype(jnp.bfloat16)
    branch_two = lax.psum(mat_mul(active_low, full_wd), "tensor")
    result = between_rows + layer_mlp * (branch_two + bias_down)
    grad_bd = column_total_sum(incoming_gradient * layer_mlp)
    grad_lm = column_total_sum(incoming_gradient * (branch_two + bias_down))
    grad_mid_low = (incoming_gradient * layer_mlp).astype(jnp.bfloat16)
    grad_wd = rows_mul(active_low, grad_mid_low)
    grad_active = back_mul(grad_mid_low, full_wd)
    gelu_value, gelu_back = jax.vjp(partial(jax.nn.gelu, approximate=False), inner)
    grad_inner = gelu_back(grad_active)[0].astype(jnp.bfloat16)
    grad_bu = column_total_sum(grad_inner)
    grad_wu = rows_mul(hidden_two, grad_inner)
    gradient_second_hidden = lax.psum(back_mul(grad_inner, full_wu), "tensor")
    gradient_gain_second = column_total_sum(gradient_second_hidden * second_centered_scaled)
    grad_s2 = column_total_sum(gradient_second_hidden)
    gradient_between_rows = incoming_gradient + layer_norm_backward(
        gradient_second_hidden, second_centered_scaled, second_inverse_deviation, second_norm_gain
    )
    grad_bo = column_total_sum(gradient_between_rows * layer_attn)
    grad_la = column_total_sum(gradient_between_rows * (branch + bias_out))
    grad_branch = (gradient_between_rows * layer_attn).astype(jnp.bfloat16)
    grad_wo = rows_mul(mixed_low, grad_branch)
    grad_mixed = back_mul(grad_branch, full_wo).astype(jnp.bfloat16)
    grad_query, grad_keys_all, grad_values_all = lax.map(
        partial(attend_backward, heads),
        (
            query_img,
            keys_all,
            values_all,
            grad_mixed.reshape(img_count, tok_count, local_width),
            log_total,
        ),
    )
    grad_keys, grad_values = (
        lax.psum_scatter(grad_keys_all, "ctx", scatter_dimension=1, tiled=True),
        lax.psum_scatter(grad_values_all, "ctx", scatter_dimension=1, tiled=True),
    )
    grad_query_low = grad_query.reshape(row_count, local_width).astype(jnp.bfloat16)
    grad_keys_low = grad_keys.reshape(row_count, local_width).astype(jnp.bfloat16)
    grad_values_low = grad_values.reshape(row_count, local_width).astype(jnp.bfloat16)
    grad_bq = column_total_sum(grad_query_low)
    grad_bv = column_total_sum(grad_values_low)
    grad_wq = rows_mul(hidden_one, grad_query_low)
    grad_wk = rows_mul(hidden_one, grad_keys_low)
    grad_wv = rows_mul(hidden_one, grad_values_low)
    head_terms = (
        back_mul(grad_query_low, full_wq)
        + back_mul(grad_keys_low, full_wk)
        + back_mul(grad_values_low, full_wv)
    )
    gradient_first_hidden = lax.psum(head_terms, "tensor")
    gradient_gain_first = column_total_sum(gradient_first_hidden * first_centered_scaled)
    grad_s1 = column_total_sum(gradient_first_hidden)
    input_gradient_rows = gradient_between_rows + layer_norm_backward(
        gradient_first_hidden, first_centered_scaled, first_inverse_deviation, first_norm_gain
    )
    (
        part_wq,
        part_wk,
        part_wv,
        part_wo,
        part_wu,
        part_wd,
        part_g1,
        part_s1,
        part_bo,
        part_la,
        part_g2,
        part_s2,
        part_bd,
        part_lm,
    ) = (
        lax.psum_scatter(grad_wq, ("shard", "ctx"), scatter_dimension=0, tiled=True),
        lax.psum_scatter(grad_wk, ("shard", "ctx"), scatter_dimension=0, tiled=True),
        lax.psum_scatter(grad_wv, ("shard", "ctx"), scatter_dimension=0, tiled=True),
        lax.psum_scatter(grad_wo, ("shard", "ctx"), scatter_dimension=1, tiled=True),
        lax.psum_scatter(grad_wu, ("shard", "ctx"), scatter_dimension=0, tiled=True),
        lax.psum_scatter(grad_wd, ("shard", "ctx"), scatter_dimension=1, tiled=True),
        lax.psum_scatter(gradient_gain_first, ("shard", "ctx"), scatter_dimension=0, tiled=True),
        lax.psum_scatter(grad_s1, ("shard", "ctx"), scatter_dimension=0, tiled=True),
        lax.psum_scatter(grad_bo, ("shard", "ctx"), scatter_dimension=0, tiled=True),
        lax.psum_scatter(grad_la, ("shard", "ctx"), scatter_dimension=0, tiled=True),
        lax.psum_scatter(gradient_gain_second, ("shard", "ctx"), scatter_dimension=0, tiled=True),
        lax.psum_scatter(grad_s2, ("shard", "ctx"), scatter_dimension=0, tiled=True),
        lax.psum_scatter(grad_bd, ("shard", "ctx"), scatter_dimension=0, tiled=True),
        lax.psum_scatter(grad_lm, ("shard", "ctx"), scatter_dimension=0, tiled=True),
    )
    (
        sum_wq,
        sum_wk,
        sum_wv,
        sum_wo,
        sum_wu,
        sum_wd,
        sum_g1,
        sum_s1,
        sum_bo,
        sum_la,
        sum_g2,
        sum_s2,
        sum_bd,
        sum_lm,
    ) = (
        lax.all_gather(part_wq, "ctx", axis=0, tiled=True),
        lax.all_gather(part_wk, "ctx", axis=0, tiled=True),
        lax.all_gather(part_wv, "ctx", axis=0, tiled=True),
        lax.all_gather(part_wo, "ctx", axis=1, tiled=True),
        lax.all_gather(part_wu, "ctx", axis=0, tiled=True),
        lax.all_gather(part_wd, "ctx", axis=1, tiled=True),
        lax.all_gather(part_g1, "ctx", axis=0, tiled=True),
        lax.all_gather(part_s1, "ctx", axis=0, tiled=True),
        lax.all_gather(part_bo, "ctx", axis=0, tiled=True),
        lax.all_gather(part_la, "ctx", axis=0, tiled=True),
        lax.all_gather(part_g2, "ctx", axis=0, tiled=True),
        lax.all_gather(part_s2, "ctx", axis=0, tiled=True),
        lax.all_gather(part_bd, "ctx", axis=0, tiled=True),
        lax.all_gather(part_lm, "ctx", axis=0, tiled=True),
    )
    sum_bq, sum_bv, sum_bu = lax.psum((grad_bq, grad_bv, grad_bu), ("shard", "ctx"))
    shape_out = (img_count, tok_count, width)
    return (
        result.reshape(shape_out),
        input_gradient_rows.reshape(shape_out),
        sum_g1,
        sum_s1,
        sum_wq,
        sum_bq,
        sum_wk,
        sum_wv,
        sum_bv,
        sum_wo,
        sum_bo,
        sum_la,
        sum_g2,
        sum_s2,
        sum_wu,
        sum_bu,
        sum_wd,
        sum_bd,
        sum_lm,
    )


def dot_of(left, right, left_dim, right_dim):
    return lax.dot_general(
        left, right, (((left_dim,), (right_dim,)), ((), ())), preferred_element_type=jnp.float32
    )


def forward_kernel(query_ref, key_ref, value_ref, mixed_ref, log_ref):
    for head in range(query_ref.shape[-1] // HD):
        lanes = slice(head * HD, (head + 1) * HD)
        query = query_ref[0, 0, :, lanes] * HD ** (-0.5)
        scores = dot_of(key_ref[0, 0, :, lanes], query, 1, 1)
        top = jnp.max(scores, 0, keepdims=True)
        expo = jnp.exp(scores - top)
        total = jnp.sum(expo, 0, keepdims=True)
        probs = (expo * (1.0 / total)).astype(jnp.bfloat16)
        mixed = dot_of(value_ref[0, 0, :, lanes], probs, 0, 0)
        mixed_ref[0, 0, :, lanes] = mixed.T.astype(jnp.bfloat16)
        log_ref[0, 0, 0, head : head + 1, :] = top + jnp.log(total)


def backward_kernel(
    query_ref, key_ref, value_ref, grad_ref, log_ref, grad_query_ref, grad_key_ref, grad_value_ref
):
    for head in range(query_ref.shape[-1] // HD):
        lanes = slice(head * HD, (head + 1) * HD)
        query = query_ref[0, 0, :, lanes] * HD ** (-0.5)
        keys = key_ref[0, 0, :, lanes]
        grad = grad_ref[0, 0, :, lanes]
        scores = dot_of(keys, query, 1, 1)
        probs = jnp.exp(scores - log_ref[0, 0, 0, head : head + 1, :])
        grad_value_ref[0, 0, :, lanes] = dot_of(probs.astype(jnp.bfloat16), grad, 1, 0).astype(
            jnp.bfloat16
        )
        grad_prob = dot_of(value_ref[0, 0, :, lanes], grad, 1, 1)
        inner = jnp.sum(probs * grad_prob, 0, keepdims=True)
        grad_score = (probs * (grad_prob - inner)).astype(jnp.bfloat16)
        grad_key_ref[0, 0, :, lanes] = dot_of(grad_score, query, 1, 0).astype(jnp.bfloat16)
        grad_query = dot_of(keys, grad_score, 0, 0) * HD ** (-0.5)
        grad_query_ref[0, 0, :, lanes] = grad_query.T.astype(jnp.bfloat16)


def attention_specs(queries, keys):
    tok_count, seq, pair = queries.shape[2], keys.shape[2], 2 * HD
    row = pl.BlockSpec((1, 1, tok_count, pair), lambda t, i, p: (t, i, 0, p))
    col = pl.BlockSpec((1, 1, seq, pair), lambda t, i, p: (t, i, 0, p))
    log = pl.BlockSpec((1, 1, 1, 2, tok_count), lambda t, i, p: (t, i, p, 0, 0))
    grid = (queries.shape[0], queries.shape[1], queries.shape[3] // pair)
    return row, col, log, grid


def attention_cost(queries, keys, products):
    pairs = queries.size * keys.shape[2]
    return pl.CostEstimate(
        flops=2 * products * pairs,
        bytes_accessed=4 * (queries.size + 2 * keys.size),
        transcendentals=pairs // HD,
    )


def attention_forward(queries, keys, values):
    row, col, log, grid = attention_specs(queries, keys)
    part, img, tok_count, width = queries.shape
    return pl.pallas_call(
        forward_kernel,
        grid=grid,
        in_specs=[row, col, col],
        out_specs=[row, log],
        out_shape=[
            jax.ShapeDtypeStruct(queries.shape, jnp.bfloat16),
            jax.ShapeDtypeStruct((part, img, width // (2 * HD), 2, tok_count), jnp.float32),
        ],
        compiler_params=pltpu.CompilerParams(vmem_limit_bytes=40 * 2**20),
        cost_estimate=attention_cost(queries, keys, 2),
    )(queries, keys, values)


def attention_backward(queries, keys, values, grad, log_total):
    row, col, log, grid = attention_specs(queries, keys)
    return pl.pallas_call(
        backward_kernel,
        grid=grid,
        in_specs=[row, col, col, row, log],
        out_specs=[row, col, col],
        out_shape=[
            jax.ShapeDtypeStruct(queries.shape, jnp.bfloat16),
            jax.ShapeDtypeStruct(keys.shape, jnp.bfloat16),
            jax.ShapeDtypeStruct(keys.shape, jnp.bfloat16),
        ],
        compiler_params=pltpu.CompilerParams(vmem_limit_bytes=40 * 2**20),
        cost_estimate=attention_cost(queries, keys, 5),
    )(queries, keys, values, grad, log_total)


ALL = ("tensor", "shard", "ctx")


def split_mul(left, right):
    return jnp.einsum("rd,tdf->trf", left, right, preferred_element_type=jnp.float32)


def split_back_mul(left, right):
    return jnp.einsum("trf,tdf->rd", left, right, preferred_element_type=jnp.float32)


def split_rows_mul(left, right):
    return jnp.einsum("rd,trf->tdf", left, right, preferred_element_type=jnp.float32).astype(
        jnp.bfloat16
    )


def gather_weight(piece, parts, at):
    rows = piece.shape[0] // parts
    mine = lax.dynamic_slice_in_dim(piece, at * rows, rows, 0)
    return lax.all_gather(mine, ALL, axis=0, tiled=True)


def reduce_weight(grad):
    width = grad.shape[-1]
    part = lax.psum_scatter(grad.reshape(-1, width), ALL, scatter_dimension=0, tiled=True)
    return lax.all_gather(part, "ctx", axis=0, tiled=True).astype(jnp.float32)


def token_split(
    tokens,
    cotangent,
    norm1_gain,
    norm1_shift,
    query_weight,
    query_bias,
    key_weight,
    value_weight,
    value_bias,
    out_weight,
    out_bias,
    scale_attn,
    norm2_gain,
    norm2_shift,
    up_weight,
    up_bias,
    down_weight,
    down_bias,
    scale_mlp,
):
    tensor_parts, ctx_parts = lax.axis_size("tensor"), lax.axis_size("ctx")
    shard_parts = lax.axis_size("shard")
    at_tensor, at_ctx, at_shard = (lax.axis_index(a) for a in ("tensor", "ctx", "shard"))
    width = tokens.shape[-1]
    head_width = query_weight.shape[1]
    img_count = tokens.shape[0] // tensor_parts
    tok_count = tokens.shape[1]
    row_count = img_count * tok_count

    cut = norm1_gain.shape[0]
    shard_vectors = [
        norm1_gain, norm1_shift, out_bias, scale_attn, norm2_gain, norm2_shift, down_bias, scale_mlp
    ]
    biases = jnp.concatenate([query_bias, value_bias, up_bias])
    packed = lax.all_gather(
        jnp.concatenate(shard_vectors + [biases]), ("tensor", "shard"), axis=0
    ).reshape(tensor_parts, shard_parts, -1).astype(jnp.float32)
    vectors = packed[0, :, : 8 * cut].reshape(shard_parts, 8, cut).transpose(1, 0, 2)
    gain1, shift1, bias_out, layer_attn, gain2, shift2, bias_down, layer_mlp = vectors.reshape(
        8, shard_parts * cut
    )
    bias_all = packed[:, 0, 8 * cut :]
    bias_query = bias_all[:, None, :head_width]
    bias_value = bias_all[:, None, head_width : 2 * head_width]
    bias_up = bias_all[:, None, 2 * head_width :]

    attn_pack = jnp.concatenate([query_weight, key_weight, value_weight, out_weight.T], 1)
    full_attn = gather_weight(attn_pack, ctx_parts, at_ctx).reshape(tensor_parts, width, -1)
    full_up = gather_weight(up_weight, ctx_parts, at_ctx).reshape(tensor_parts, width, -1)
    full_down = gather_weight(down_weight.T, ctx_parts, at_ctx).reshape(tensor_parts, width, -1)
    full_qkv, full_out = full_attn[:, :, : 3 * head_width], full_attn[:, :, 3 * head_width :]

    def own(values):
        rows = lax.dynamic_slice_in_dim(values, at_tensor * img_count, img_count, 0)
        return rows.astype(jnp.float32).reshape(row_count, width)

    input_rows, incoming = own(tokens), own(cotangent)
    h1, n1, r1 = layer_norm_forward(input_rows, gain1, shift1)
    h1 = h1.astype(jnp.bfloat16)
    qkv = split_mul(h1, full_qkv)
    by_image = (tensor_parts, img_count, tok_count)
    queries = (qkv[:, :, :head_width] + bias_query).astype(jnp.bfloat16)
    queries = queries.reshape(*by_image, head_width)
    keys = qkv[:, :, head_width : 2 * head_width].astype(jnp.bfloat16)
    values = (qkv[:, :, 2 * head_width :] + bias_value).astype(jnp.bfloat16)
    keys_all, values_all = (
        lax.all_gather(part.reshape(*by_image, head_width), "ctx", axis=2, tiled=True)
        for part in (keys, values)
    )
    mixed, log_total = attention_forward(queries, keys_all, values_all)
    mixed_rows = mixed.reshape(tensor_parts, row_count, head_width)
    branch = split_back_mul(mixed_rows, full_out)
    between = input_rows + layer_attn * (branch + bias_out)
    h2, n2, r2 = layer_norm_forward(between, gain2, shift2)
    h2 = h2.astype(jnp.bfloat16)
    inner = split_mul(h2, full_up) + bias_up
    active = jax.nn.gelu(inner, approximate=False).astype(jnp.bfloat16)
    branch_two = split_back_mul(active, full_down)
    result = between + layer_mlp * (branch_two + bias_down)

    grad_bd = column_total_sum(incoming * layer_mlp)
    grad_lm = column_total_sum(incoming * (branch_two + bias_down))
    grad_mid = (incoming * layer_mlp).astype(jnp.bfloat16)
    grad_wd = reduce_weight(split_rows_mul(grad_mid, active))
    grad_active = split_mul(grad_mid, full_down)
    _, gelu_back = jax.vjp(partial(jax.nn.gelu, approximate=False), inner)
    grad_inner = gelu_back(grad_active)[0].astype(jnp.bfloat16)
    grad_bu = jnp.sum(grad_inner.astype(jnp.float32), 1)
    grad_wu = reduce_weight(split_rows_mul(h2, grad_inner))
    grad_h2 = split_back_mul(grad_inner, full_up)
    grad_g2 = column_total_sum(grad_h2 * n2)
    grad_s2 = column_total_sum(grad_h2)
    grad_between = incoming + layer_norm_backward(grad_h2, n2, r2, gain2)
    grad_bo = column_total_sum(grad_between * layer_attn)
    grad_la = column_total_sum(grad_between * (branch + bias_out))
    grad_branch = (grad_between * layer_attn).astype(jnp.bfloat16)
    grad_wo = split_rows_mul(grad_branch, mixed_rows)
    grad_mixed = split_mul(grad_branch, full_out).astype(jnp.bfloat16)
    grad_query, grad_keys, grad_values = attention_backward(
        queries, keys_all, values_all, grad_mixed.reshape(*by_image, head_width), log_total
    )
    grad_keys, grad_values = (
        lax.psum_scatter(part, "ctx", scatter_dimension=2, tiled=True)
        for part in (grad_keys, grad_values)
    )
    grad_qkv = jnp.concatenate([grad_query, grad_keys, grad_values], -1)
    grad_qkv = grad_qkv.reshape(tensor_parts, row_count, 3 * head_width)
    grad_bqv = jnp.sum(grad_qkv.astype(jnp.float32), 1)
    grad_attn = reduce_weight(jnp.concatenate([split_rows_mul(h1, grad_qkv), grad_wo], -1))
    grad_h1 = split_back_mul(grad_qkv, full_qkv)
    grad_g1 = column_total_sum(grad_h1 * n1)
    grad_s1 = column_total_sum(grad_h1)
    input_grad = grad_between + layer_norm_backward(grad_h1, n1, r1, gain1)

    def spread(rows):
        rows = rows.astype(jnp.bfloat16).reshape(img_count, tok_count, width)
        return lax.all_gather(rows, "tensor", axis=0, tiled=True).astype(jnp.float32)

    vector_grads = [grad_g1, grad_s1, grad_bo, grad_la, grad_g2, grad_s2, grad_bd, grad_lm]
    bias_grads = jnp.concatenate(
        [grad_bqv[:, :head_width], grad_bqv[:, 2 * head_width :], grad_bu], 1
    )
    summed = lax.psum(jnp.concatenate(vector_grads + [bias_grads.reshape(-1)]), ALL)
    vector_sums = lax.dynamic_slice_in_dim(
        summed[: 8 * width].reshape(8, width), at_shard * cut, cut, 1
    )
    sum_g1, sum_s1, sum_bo, sum_la, sum_g2, sum_s2, sum_bd, sum_lm = vector_sums
    bias_sums = lax.dynamic_index_in_dim(
        summed[8 * width :].reshape(tensor_parts, -1), at_tensor, 0, keepdims=False
    )
    return (
        spread(result),
        spread(input_grad),
        sum_g1,
        sum_s1,
        grad_attn[:, :head_width],
        bias_sums[:head_width],
        grad_attn[:, head_width : 2 * head_width],
        grad_attn[:, 2 * head_width : 3 * head_width],
        bias_sums[head_width : 2 * head_width],
        grad_attn[:, 3 * head_width :].T,
        sum_bo,
        sum_la,
        sum_g2,
        sum_s2,
        grad_wu,
        bias_sums[2 * head_width :],
        grad_wd.T,
        sum_bd,
        sum_lm,
    )


def per_device(*arrays):
    if arrays[0].shape[0] % lax.axis_size("tensor") == 0:
        return token_split(*arrays)
    return local(*arrays)


def solution(mesh):
    in_specs = (
        P("shard", "ctx", None),
        P("shard", "ctx", None),
        P("shard"),
        P("shard"),
        P("shard", "tensor"),
        P("tensor"),
        P("shard", "tensor"),
        P("shard", "tensor"),
        P("tensor"),
        P("tensor", "shard"),
        P("shard"),
        P("shard"),
        P("shard"),
        P("shard"),
        P("shard", "tensor"),
        P("tensor"),
        P("tensor", "shard"),
        P("shard"),
        P("shard"),
    )
    out_specs = (
        P("shard", "ctx", None),
        P("shard", "ctx", None),
        P("shard"),
        P("shard"),
        P("shard", "tensor"),
        P("tensor"),
        P("shard", "tensor"),
        P("shard", "tensor"),
        P("tensor"),
        P("tensor", "shard"),
        P("shard"),
        P("shard"),
        P("shard"),
        P("shard"),
        P("shard", "tensor"),
        P("tensor"),
        P("tensor", "shard"),
        P("shard"),
        P("shard"),
    )
    return jax.shard_map(per_device, mesh=mesh, in_specs=in_specs, out_specs=out_specs, check_vma=False)
```

```python
from functools import partial

import jax
import jax.numpy as jnp
from jax import lax
from jax.experimental import pallas as pl
from jax.experimental.pallas import tpu as pltpu
from jax.sharding import PartitionSpec as P

HD = 64


EPSILON = 1e-06


def layer_norm_forward(values, norm_gain, norm_shift):
    center = values - jnp.mean(values, -1, keepdims=True)
    inverse = lax.rsqrt(jnp.mean(center * center, -1, keepdims=True) + EPSILON)
    normed = center * inverse
    return (normed * norm_gain + norm_shift, normed, inverse)


def layer_norm_backward(incoming_gradient, normed, inverse, norm_gain):
    scaled = incoming_gradient * norm_gain
    return inverse * (
        scaled
        - jnp.mean(scaled, -1, keepdims=True)
        - normed * jnp.mean(scaled * normed, -1, keepdims=True)
    )


def mat_mul(left, right):
    return jnp.dot(left, right, preferred_element_type=jnp.float32)


def rows_mul(left, right):
    return jnp.einsum("rd,re->de", left, right, preferred_element_type=jnp.float32)


def back_mul(left, right):
    return jnp.einsum("re,de->rd", left, right, preferred_element_type=jnp.float32)


def column_total_sum(values):
    return jnp.sum(values.astype(jnp.float32), 0)


def split_heads(values, heads):
    return values.reshape(values.shape[0], heads, HD)


def scores_of(queries, keys_all, heads):
    return jnp.einsum(
        "qhe,khe->hqk",
        split_heads(queries, heads),
        split_heads(keys_all, heads),
        preferred_element_type=jnp.float32,
    ) * HD ** (-0.5)


def attend_forward(heads, args):
    queries, keys_all, values_all = args
    scores = scores_of(queries, keys_all, heads)
    row_top = jnp.max(scores, -1, keepdims=True)
    expo = jnp.exp(scores - row_top)
    total = jnp.sum(expo, -1, keepdims=True)
    probs = (expo / total).astype(jnp.bfloat16)
    mixed = jnp.einsum(
        "hqk,khe->qhe", probs, split_heads(values_all, heads), preferred_element_type=jnp.float32
    )
    log_total = (row_top + jnp.log(total))[..., 0]
    return (mixed.reshape(queries.shape[0], heads * HD), log_total)


def attend_backward(heads, args):
    queries, keys_all, values_all, incoming_gradient, log_total = args
    scores = scores_of(queries, keys_all, heads)
    probs = jnp.exp(scores - log_total[..., None])
    up_heads = split_heads(incoming_gradient, heads)
    grad_value = jnp.einsum(
        "hqk,qhe->khe", probs.astype(jnp.bfloat16), up_heads, preferred_element_type=jnp.float32
    )
    grad_prob = jnp.einsum(
        "qhe,khe->hqk", up_heads, split_heads(values_all, heads), preferred_element_type=jnp.float32
    )
    grad_score = (probs * (grad_prob - jnp.sum(probs * grad_prob, -1, keepdims=True))).astype(
        jnp.bfloat16
    )
    grad_query = jnp.einsum(
        "hqk,khe->qhe", grad_score, split_heads(keys_all, heads), preferred_element_type=jnp.float32
    ) * HD ** (-0.5)
    grad_key = jnp.einsum(
        "hqk,qhe->khe", grad_score, split_heads(queries, heads), preferred_element_type=jnp.float32
    ) * HD ** (-0.5)
    width = heads * HD
    return (
        grad_query.reshape(queries.shape[0], width),
        grad_key.reshape(keys_all.shape[0], width),
        grad_value.reshape(keys_all.shape[0], width),
    )


def local(
    tokens,
    cotangent,
    norm1_gain,
    norm1_shift,
    query_weight,
    query_bias,
    key_weight,
    value_weight,
    value_bias,
    out_weight,
    out_bias,
    scale_attn,
    norm2_gain,
    norm2_shift,
    up_weight,
    up_bias,
    down_weight,
    down_bias,
    scale_mlp,
):
    full_g1, full_s1, full_wq, full_wk, full_wv, full_wo, full_bo, full_la = (
        lax.all_gather(norm1_gain, "shard", axis=0, tiled=True),
        lax.all_gather(norm1_shift, "shard", axis=0, tiled=True),
        lax.all_gather(query_weight, "shard", axis=0, tiled=True),
        lax.all_gather(key_weight, "shard", axis=0, tiled=True),
        lax.all_gather(value_weight, "shard", axis=0, tiled=True),
        lax.all_gather(out_weight, "shard", axis=1, tiled=True),
        lax.all_gather(out_bias, "shard", axis=0, tiled=True),
        lax.all_gather(scale_attn, "shard", axis=0, tiled=True),
    )
    full_g2, full_s2, full_wu, full_wd, full_bd, full_lm = (
        lax.all_gather(norm2_gain, "shard", axis=0, tiled=True),
        lax.all_gather(norm2_shift, "shard", axis=0, tiled=True),
        lax.all_gather(up_weight, "shard", axis=0, tiled=True),
        lax.all_gather(down_weight, "shard", axis=1, tiled=True),
        lax.all_gather(down_bias, "shard", axis=0, tiled=True),
        lax.all_gather(scale_mlp, "shard", axis=0, tiled=True),
    )
    first_norm_gain = full_g1.astype(jnp.float32)
    first_norm_offset = full_s1.astype(jnp.float32)
    second_norm_gain = full_g2.astype(jnp.float32)
    second_norm_offset = full_s2.astype(jnp.float32)
    bias_out = full_bo.astype(jnp.float32)
    layer_attn = full_la.astype(jnp.float32)
    bias_down = full_bd.astype(jnp.float32)
    layer_mlp = full_lm.astype(jnp.float32)
    img_count, tok_count, width = tokens.shape
    row_count = img_count * tok_count
    local_width = full_wq.shape[1]
    heads = local_width // HD
    input_rows = tokens.astype(jnp.float32).reshape(row_count, width)
    incoming_gradient = cotangent.astype(jnp.float32).reshape(row_count, width)
    first_normalized_rows, first_centered_scaled, first_inverse_deviation = layer_norm_forward(
        input_rows, first_norm_gain, first_norm_offset
    )
    hidden_one = first_normalized_rows.astype(jnp.bfloat16)
    queries = (mat_mul(hidden_one, full_wq) + query_bias.astype(jnp.float32)).astype(jnp.bfloat16)
    keys_local = mat_mul(hidden_one, full_wk).astype(jnp.bfloat16)
    values_local = (mat_mul(hidden_one, full_wv) + value_bias.astype(jnp.float32)).astype(
        jnp.bfloat16
    )
    keys_all, values_all = (
        lax.all_gather(
            keys_local.reshape(img_count, tok_count, local_width), "ctx", axis=1, tiled=True
        ),
        lax.all_gather(
            values_local.reshape(img_count, tok_count, local_width), "ctx", axis=1, tiled=True
        ),
    )
    query_img = queries.reshape(img_count, tok_count, local_width)
    mixed, log_total = lax.map(partial(attend_forward, heads), (query_img, keys_all, values_all))
    mixed_low = mixed.reshape(row_count, local_width).astype(jnp.bfloat16)
    branch = lax.psum(mat_mul(mixed_low, full_wo), "tensor")
    between_rows = input_rows + layer_attn * (branch + bias_out)
    second_normalized_rows, second_centered_scaled, second_inverse_deviation = layer_norm_forward(
        between_rows, second_norm_gain, second_norm_offset
    )
    hidden_two = second_normalized_rows.astype(jnp.bfloat16)
    inner = mat_mul(hidden_two, full_wu) + up_bias.astype(jnp.float32)
    active_low = jax.nn.gelu(inner, approximate=False).astype(jnp.bfloat16)
    branch_two = lax.psum(mat_mul(active_low, full_wd), "tensor")
    result = between_rows + layer_mlp * (branch_two + bias_down)
    grad_bd = column_total_sum(incoming_gradient * layer_mlp)
    grad_lm = column_total_sum(incoming_gradient * (branch_two + bias_down))
    grad_mid_low = (incoming_gradient * layer_mlp).astype(jnp.bfloat16)
    grad_wd = rows_mul(active_low, grad_mid_low)
    grad_active = back_mul(grad_mid_low, full_wd)
    gelu_value, gelu_back = jax.vjp(partial(jax.nn.gelu, approximate=False), inner)
    grad_inner = gelu_back(grad_active)[0].astype(jnp.bfloat16)
    grad_bu = column_total_sum(grad_inner)
    grad_wu = rows_mul(hidden_two, grad_inner)
    gradient_second_hidden = lax.psum(back_mul(grad_inner, full_wu), "tensor")
    gradient_gain_second = column_total_sum(gradient_second_hidden * second_centered_scaled)
    grad_s2 = column_total_sum(gradient_second_hidden)
    gradient_between_rows = incoming_gradient + layer_norm_backward(
        gradient_second_hidden, second_centered_scaled, second_inverse_deviation, second_norm_gain
    )
    grad_bo = column_total_sum(gradient_between_rows * layer_attn)
    grad_la = column_total_sum(gradient_between_rows * (branch + bias_out))
    grad_branch = (gradient_between_rows * layer_attn).astype(jnp.bfloat16)
    grad_wo = rows_mul(mixed_low, grad_branch)
    grad_mixed = back_mul(grad_branch, full_wo).astype(jnp.bfloat16)
    grad_query, grad_keys_all, grad_values_all = lax.map(
        partial(attend_backward, heads),
        (
            query_img,
            keys_all,
            values_all,
            grad_mixed.reshape(img_count, tok_count, local_width),
            log_total,
        ),
    )
    grad_keys, grad_values = (
        lax.psum_scatter(grad_keys_all, "ctx", scatter_dimension=1, tiled=True),
        lax.psum_scatter(grad_values_all, "ctx", scatter_dimension=1, tiled=True),
    )
    grad_query_low = grad_query.reshape(row_count, local_width).astype(jnp.bfloat16)
    grad_keys_low = grad_keys.reshape(row_count, local_width).astype(jnp.bfloat16)
    grad_values_low = grad_values.reshape(row_count, local_width).astype(jnp.bfloat16)
    grad_bq = column_total_sum(grad_query_low)
    grad_bv = column_total_sum(grad_values_low)
    grad_wq = rows_mul(hidden_one, grad_query_low)
    grad_wk = rows_mul(hidden_one, grad_keys_low)
    grad_wv = rows_mul(hidden_one, grad_values_low)
    head_terms = (
        back_mul(grad_query_low, full_wq)
        + back_mul(grad_keys_low, full_wk)
        + back_mul(grad_values_low, full_wv)
    )
    gradient_first_hidden = lax.psum(head_terms, "tensor")
    gradient_gain_first = column_total_sum(gradient_first_hidden * first_centered_scaled)
    grad_s1 = column_total_sum(gradient_first_hidden)
    input_gradient_rows = gradient_between_rows + layer_norm_backward(
        gradient_first_hidden, first_centered_scaled, first_inverse_deviation, first_norm_gain
    )
    (
        part_wq,
        part_wk,
        part_wv,
        part_wo,
        part_wu,
        part_wd,
        part_g1,
        part_s1,
        part_bo,
        part_la,
        part_g2,
        part_s2,
        part_bd,
        part_lm,
    ) = (
        lax.psum_scatter(grad_wq, ("shard", "ctx"), scatter_dimension=0, tiled=True),
        lax.psum_scatter(grad_wk, ("shard", "ctx"), scatter_dimension=0, tiled=True),
        lax.psum_scatter(grad_wv, ("shard", "ctx"), scatter_dimension=0, tiled=True),
        lax.psum_scatter(grad_wo, ("shard", "ctx"), scatter_dimension=1, tiled=True),
        lax.psum_scatter(grad_wu, ("shard", "ctx"), scatter_dimension=0, tiled=True),
        lax.psum_scatter(grad_wd, ("shard", "ctx"), scatter_dimension=1, tiled=True),
        lax.psum_scatter(gradient_gain_first, ("shard", "ctx"), scatter_dimension=0, tiled=True),
        lax.psum_scatter(grad_s1, ("shard", "ctx"), scatter_dimension=0, tiled=True),
        lax.psum_scatter(grad_bo, ("shard", "ctx"), scatter_dimension=0, tiled=True),
        lax.psum_scatter(grad_la, ("shard", "ctx"), scatter_dimension=0, tiled=True),
        lax.psum_scatter(gradient_gain_second, ("shard", "ctx"), scatter_dimension=0, tiled=True),
        lax.psum_scatter(grad_s2, ("shard", "ctx"), scatter_dimension=0, tiled=True),
        lax.psum_scatter(grad_bd, ("shard", "ctx"), scatter_dimension=0, tiled=True),
        lax.psum_scatter(grad_lm, ("shard", "ctx"), scatter_dimension=0, tiled=True),
    )
    (
        sum_wq,
        sum_wk,
        sum_wv,
        sum_wo,
        sum_wu,
        sum_wd,
        sum_g1,
        sum_s1,
        sum_bo,
        sum_la,
        sum_g2,
        sum_s2,
        sum_bd,
        sum_lm,
    ) = (
        lax.all_gather(part_wq, "ctx", axis=0, tiled=True),
        lax.all_gather(part_wk, "ctx", axis=0, tiled=True),
        lax.all_gather(part_wv, "ctx", axis=0, tiled=True),
        lax.all_gather(part_wo, "ctx", axis=1, tiled=True),
        lax.all_gather(part_wu, "ctx", axis=0, tiled=True),
        lax.all_gather(part_wd, "ctx", axis=1, tiled=True),
        lax.all_gather(part_g1, "ctx", axis=0, tiled=True),
        lax.all_gather(part_s1, "ctx", axis=0, tiled=True),
        lax.all_gather(part_bo, "ctx", axis=0, tiled=True),
        lax.all_gather(part_la, "ctx", axis=0, tiled=True),
        lax.all_gather(part_g2, "ctx", axis=0, tiled=True),
        lax.all_gather(part_s2, "ctx", axis=0, tiled=True),
        lax.all_gather(part_bd, "ctx", axis=0, tiled=True),
        lax.all_gather(part_lm, "ctx", axis=0, tiled=True),
    )
    sum_bq, sum_bv, sum_bu = lax.psum((grad_bq, grad_bv, grad_bu), ("shard", "ctx"))
    shape_out = (img_count, tok_count, width)
    return (
        result.reshape(shape_out),
        input_gradient_rows.reshape(shape_out),
        sum_g1,
        sum_s1,
        sum_wq,
        sum_bq,
        sum_wk,
        sum_wv,
        sum_bv,
        sum_wo,
        sum_bo,
        sum_la,
        sum_g2,
        sum_s2,
        sum_wu,
        sum_bu,
        sum_wd,
        sum_bd,
        sum_lm,
    )


def dot_of(left, right, left_dim, right_dim):
    return lax.dot_general(
        left, right, (((left_dim,), (right_dim,)), ((), ())), preferred_element_type=jnp.float32
    )


def head_lanes(head, width):
    return slice(head * HD, (head + 1) * HD), slice(width + head * HD, width + (head + 1) * HD)


def forward_kernel(query_ref, pair_ref, mixed_ref, log_ref):
    width = query_ref.shape[-1]
    for head in range(width // HD):
        lanes, value_lanes = head_lanes(head, width)
        query = query_ref[0, 0, :, lanes] * HD ** (-0.5)
        scores = dot_of(pair_ref[0, 0, :, lanes], query, 1, 1)
        top = jnp.max(scores, 0, keepdims=True)
        expo = jnp.exp(scores - top)
        total = jnp.sum(expo, 0, keepdims=True)
        probs = (expo * (1.0 / total)).astype(jnp.bfloat16)
        mixed = dot_of(pair_ref[0, 0, :, value_lanes], probs, 0, 0)
        mixed_ref[0, 0, :, lanes] = mixed.T.astype(jnp.bfloat16)
        log_ref[0, 0, head : head + 1, :] = top + jnp.log(total)


def backward_kernel(query_ref, pair_ref, grad_ref, log_ref, grad_query_ref, grad_pair_ref):
    tok_count, width = query_ref.shape[-2:]

    def store_pair(lanes, total):
        for part in range(grad_pair_ref.shape[0]):
            rows = total[part * tok_count : (part + 1) * tok_count]
            grad_pair_ref[part, 0, 0, :, lanes] = rows.astype(jnp.bfloat16)

    for head in range(width // HD):
        lanes, value_lanes = head_lanes(head, width)
        query = query_ref[0, 0, :, lanes] * HD ** (-0.5)
        keys = pair_ref[0, 0, :, lanes]
        grad = grad_ref[0, 0, :, lanes]
        scores = dot_of(keys, query, 1, 1)
        probs = jnp.exp(scores - log_ref[0, 0, head : head + 1, :])
        store_pair(value_lanes, dot_of(probs.astype(jnp.bfloat16), grad, 1, 0))
        grad_prob = dot_of(pair_ref[0, 0, :, value_lanes], grad, 1, 1)
        inner = jnp.sum(probs * grad_prob, 0, keepdims=True)
        grad_score = (probs * (grad_prob - inner)).astype(jnp.bfloat16)
        store_pair(lanes, dot_of(grad_score, query, 1, 0))
        grad_query = dot_of(keys, grad_score, 0, 0) * HD ** (-0.5)
        grad_query_ref[0, 0, :, lanes] = grad_query.T.astype(jnp.bfloat16)


def attention_call(kernel, products, queries, pair, more, outs, out_specs, more_specs):
    part, img, tok_count, width = queries.shape
    scores = queries.size * pair.shape[2]
    row = pl.BlockSpec((1, 1, tok_count, width), lambda t, i: (t, i, 0, 0))
    col = pl.BlockSpec((1, 1) + pair.shape[2:], lambda t, i: (t, i, 0, 0))
    return pl.pallas_call(
        kernel,
        grid=(part, img),
        in_specs=[row, col] + more_specs,
        out_specs=[row] + out_specs,
        out_shape=[jax.ShapeDtypeStruct(queries.shape, jnp.bfloat16)] + outs,
        compiler_params=pltpu.CompilerParams(vmem_limit_bytes=48 * 2**20),
        cost_estimate=pl.CostEstimate(
            flops=2 * products * scores,
            bytes_accessed=4 * (queries.size + pair.size),
            transcendentals=scores // HD,
        ),
    )(queries, pair, *more)


def log_layout(queries):
    part, img, tok_count, width = queries.shape
    dims = (part, img, width // HD, tok_count)
    return dims, pl.BlockSpec((1, 1) + dims[2:], lambda t, i: (t, i, 0, 0))


def attention_forward(queries, pair):
    dims, log = log_layout(queries)
    outs = [jax.ShapeDtypeStruct(dims, jnp.float32)]
    return attention_call(forward_kernel, 2, queries, pair, (), outs, [log], [])


def attention_backward(queries, pair, grad, log_total):
    part, img, tok_count, width = queries.shape
    _, log = log_layout(queries)
    row = pl.BlockSpec((1, 1, tok_count, width), lambda t, i: (t, i, 0, 0))
    blocks = pair.shape[2] // tok_count
    outs = [jax.ShapeDtypeStruct((blocks, part, img, tok_count, 2 * width), jnp.bfloat16)]
    split = pl.BlockSpec((blocks, 1, 1, tok_count, 2 * width), lambda t, i: (0, t, i, 0, 0))
    return attention_call(
        backward_kernel, 5, queries, pair, (grad, log_total), outs, [split], [row, log]
    )


ALL = ("tensor", "shard", "ctx")


def split_mul(left, right):
    return jnp.einsum("rd,tdf->trf", left, right, preferred_element_type=jnp.float32)


def split_back_mul(left, right):
    return jnp.einsum("trf,tdf->rd", left, right, preferred_element_type=jnp.float32)


def split_rows_mul(left, right):
    return jnp.einsum("rd,trf->tdf", left, right, preferred_element_type=jnp.float32).astype(
        jnp.bfloat16
    )


def gather_weight(piece, parts, at):
    rows = piece.shape[0] // parts
    mine = lax.dynamic_slice_in_dim(piece, at * rows, rows, 0)
    return lax.all_gather(mine, ALL, axis=0, tiled=True)


def reduce_weights(grads, parts):
    cuts = [grad.reshape(parts, -1, grad.shape[-1]) for grad in grads]
    part = lax.psum_scatter(
        jnp.concatenate(cuts, 1), ALL, scatter_dimension=0, tiled=True
    )
    full = lax.all_gather(part, "ctx", axis=0, tiled=True)
    rows = cuts[0].shape[1]
    return [
        full[:, at * rows : (at + 1) * rows].reshape(-1, full.shape[-1]).astype(jnp.float32)
        for at in range(len(cuts))
    ]


def token_split(
    tokens,
    cotangent,
    norm1_gain,
    norm1_shift,
    query_weight,
    query_bias,
    key_weight,
    value_weight,
    value_bias,
    out_weight,
    out_bias,
    scale_attn,
    norm2_gain,
    norm2_shift,
    up_weight,
    up_bias,
    down_weight,
    down_bias,
    scale_mlp,
):
    tensor_parts, ctx_parts = lax.axis_size("tensor"), lax.axis_size("ctx")
    shard_parts = lax.axis_size("shard")
    at_tensor, at_ctx, at_shard = (lax.axis_index(a) for a in ("tensor", "ctx", "shard"))
    width = tokens.shape[-1]
    head_width = query_weight.shape[1]
    img_count = tokens.shape[0] // tensor_parts
    tok_count = tokens.shape[1]
    row_count = img_count * tok_count

    cut = norm1_gain.shape[0]
    shard_vectors = [
        norm1_gain, norm1_shift, out_bias, scale_attn, norm2_gain, norm2_shift, down_bias, scale_mlp
    ]
    biases = jnp.concatenate([query_bias, value_bias, up_bias])
    packed = lax.all_gather(
        jnp.concatenate(shard_vectors + [biases]), ("tensor", "shard"), axis=0
    ).reshape(tensor_parts, shard_parts, -1).astype(jnp.float32)
    vectors = packed[0, :, : 8 * cut].reshape(shard_parts, 8, cut).transpose(1, 0, 2)
    gain1, shift1, bias_out, layer_attn, gain2, shift2, bias_down, layer_mlp = vectors.reshape(
        8, shard_parts * cut
    )
    bias_all = packed[:, 0, 8 * cut :]
    bias_query = bias_all[:, None, :head_width]
    bias_value = bias_all[:, None, head_width : 2 * head_width]
    bias_up = bias_all[:, None, 2 * head_width :]

    attn_pack = jnp.concatenate([query_weight, key_weight, value_weight, out_weight.T], 1)
    full_attn = gather_weight(attn_pack, ctx_parts, at_ctx).reshape(tensor_parts, width, -1)
    full_qkv, full_out = full_attn[:, :, : 3 * head_width], full_attn[:, :, 3 * head_width :]

    def own(values):
        rows = lax.dynamic_slice_in_dim(values, at_tensor * img_count, img_count, 0)
        return rows.astype(jnp.float32).reshape(row_count, width)

    input_rows, incoming = own(tokens), own(cotangent)
    h1, n1, r1 = layer_norm_forward(input_rows, gain1, shift1)
    h1 = h1.astype(jnp.bfloat16)
    qkv = split_mul(h1, full_qkv)
    by_image = (tensor_parts, img_count, tok_count)
    queries = (qkv[:, :, :head_width] + bias_query).astype(jnp.bfloat16)
    queries = queries.reshape(*by_image, head_width)
    bias_pair = jnp.concatenate([jnp.zeros_like(bias_value), bias_value], -1)
    pair = (qkv[:, :, head_width:] + bias_pair).astype(jnp.bfloat16)
    pair = lax.all_gather(pair.reshape(*by_image, -1), "ctx", axis=2, tiled=True)
    pair, up_weight, down_weight = lax.optimization_barrier((pair, up_weight, down_weight))
    full_up = gather_weight(up_weight, ctx_parts, at_ctx).reshape(tensor_parts, width, -1)
    full_down = gather_weight(down_weight.T, ctx_parts, at_ctx).reshape(tensor_parts, width, -1)
    mixed, log_total = attention_forward(queries, pair)
    mixed_rows = mixed.reshape(tensor_parts, row_count, head_width)
    branch = split_back_mul(mixed_rows, full_out)
    between = input_rows + layer_attn * (branch + bias_out)
    h2, n2, r2 = layer_norm_forward(between, gain2, shift2)
    h2 = h2.astype(jnp.bfloat16)
    inner = split_mul(h2, full_up) + bias_up
    active = jax.nn.gelu(inner, approximate=False).astype(jnp.bfloat16)
    branch_two = split_back_mul(active, full_down)
    result = between + layer_mlp * (branch_two + bias_down)

    def spread(rows):
        rows = rows.astype(jnp.bfloat16).reshape(img_count, tok_count, width)
        return lax.all_gather(rows, "tensor", axis=0, tiled=True)

    block_out = spread(result)
    grad_bd = column_total_sum(incoming * layer_mlp)
    grad_lm = column_total_sum(incoming * (branch_two + bias_down))
    grad_mid = (incoming * layer_mlp).astype(jnp.bfloat16)
    grad_wd = split_rows_mul(grad_mid, active)
    grad_active = split_mul(grad_mid, full_down)
    _, gelu_back = jax.vjp(partial(jax.nn.gelu, approximate=False), inner)
    grad_inner = gelu_back(grad_active)[0].astype(jnp.bfloat16)
    grad_bu = jnp.sum(grad_inner.astype(jnp.float32), 1)
    grad_wu = split_rows_mul(h2, grad_inner)
    grad_h2 = split_back_mul(grad_inner, full_up)
    grad_g2 = column_total_sum(grad_h2 * n2)
    grad_s2 = column_total_sum(grad_h2)
    grad_between = incoming + layer_norm_backward(grad_h2, n2, r2, gain2)
    grad_bo = column_total_sum(grad_between * layer_attn)
    grad_la = column_total_sum(grad_between * (branch + bias_out))
    grad_branch = (grad_between * layer_attn).astype(jnp.bfloat16)
    grad_wo = split_rows_mul(grad_branch, mixed_rows)
    grad_mixed = split_mul(grad_branch, full_out).astype(jnp.bfloat16)
    grad_query, grad_pair = attention_backward(
        queries, pair, grad_mixed.reshape(*by_image, head_width), log_total
    )
    grad_pair, block_out = lax.optimization_barrier((grad_pair, block_out))
    grad_pair = lax.psum_scatter(grad_pair, "ctx", scatter_dimension=0, tiled=True)
    grad_query = grad_query.reshape(tensor_parts, row_count, head_width)
    grad_pair = grad_pair.reshape(tensor_parts, row_count, 2 * head_width)
    grad_bq = jnp.sum(grad_query.astype(jnp.float32), 1)
    grad_bv = jnp.sum(grad_pair[:, :, head_width:].astype(jnp.float32), 1)
    grad_attn = jnp.concatenate(
        [split_rows_mul(h1, grad_query), split_rows_mul(h1, grad_pair), grad_wo], -1
    )
    grad_h1 = split_back_mul(grad_query, full_qkv[:, :, :head_width]) + split_back_mul(
        grad_pair, full_qkv[:, :, head_width:]
    )
    grad_attn, grad_wu, grad_wd = reduce_weights(
        [grad_attn, grad_wu, grad_wd], tensor_parts * shard_parts * ctx_parts
    )
    grad_g1 = column_total_sum(grad_h1 * n1)
    grad_s1 = column_total_sum(grad_h1)
    input_grad = grad_between + layer_norm_backward(grad_h1, n1, r1, gain1)

    vector_grads = [grad_g1, grad_s1, grad_bo, grad_la, grad_g2, grad_s2, grad_bd, grad_lm]
    bias_grads = jnp.concatenate([grad_bq, grad_bv, grad_bu], 1)
    summed = lax.psum(jnp.concatenate(vector_grads + [bias_grads.reshape(-1)]), ALL)
    vector_sums = lax.dynamic_slice_in_dim(
        summed[: 8 * width].reshape(8, width), at_shard * cut, cut, 1
    )
    sum_g1, sum_s1, sum_bo, sum_la, sum_g2, sum_s2, sum_bd, sum_lm = vector_sums
    bias_sums = lax.dynamic_index_in_dim(
        summed[8 * width :].reshape(tensor_parts, -1), at_tensor, 0, keepdims=False
    )
    return (
        block_out.astype(jnp.float32),
        spread(input_grad).astype(jnp.float32),
        sum_g1,
        sum_s1,
        grad_attn[:, :head_width],
        bias_sums[:head_width],
        grad_attn[:, head_width : 2 * head_width],
        grad_attn[:, 2 * head_width : 3 * head_width],
        bias_sums[head_width : 2 * head_width],
        grad_attn[:, 3 * head_width :].T,
        sum_bo,
        sum_la,
        sum_g2,
        sum_s2,
        grad_wu,
        bias_sums[2 * head_width :],
        grad_wd.T,
        sum_bd,
        sum_lm,
    )


def per_device(*arrays):
    if arrays[0].shape[0] % lax.axis_size("tensor") == 0:
        return token_split(*arrays)
    return local(*arrays)


def solution(mesh):
    in_specs = (
        P("shard", "ctx", None),
        P("shard", "ctx", None),
        P("shard"),
        P("shard"),
        P("shard", "tensor"),
        P("tensor"),
        P("shard", "tensor"),
        P("shard", "tensor"),
        P("tensor"),
        P("tensor", "shard"),
        P("shard"),
        P("shard"),
        P("shard"),
        P("shard"),
        P("shard", "tensor"),
        P("tensor"),
        P("tensor", "shard"),
        P("shard"),
        P("shard"),
    )
    out_specs = (
        P("shard", "ctx", None),
        P("shard", "ctx", None),
        P("shard"),
        P("shard"),
        P("shard", "tensor"),
        P("tensor"),
        P("shard", "tensor"),
        P("shard", "tensor"),
        P("tensor"),
        P("tensor", "shard"),
        P("shard"),
        P("shard"),
        P("shard"),
        P("shard"),
        P("shard", "tensor"),
        P("tensor"),
        P("tensor", "shard"),
        P("shard"),
        P("shard"),
    )
    return jax.shard_map(per_device, mesh=mesh, in_specs=in_specs, out_specs=out_specs, check_vma=False)
```
